256 devices in a mesh: ctx: 8 (over z), dp: 32 (over y, x, core).
Axes of the slice: x: 4, y: 4, z: 8, core: 2. Of those that a mesh axis runs over, the one named last changes fastest.
Arguments:
- layer_input: bfloat16 [32, 1024, 8192], P('dp', 'ctx'), may hold values from -6 to 6
- query: bfloat16 [32, 1024, 4096], P('dp', 'ctx'), may hold values from -6 to 6
- key: bfloat16 [32, 1024, 512], P('dp', 'ctx'), may hold values from -6 to 6
- value: bfloat16 [32, 1024, 512], P('dp', 'ctx'), may hold values from -6 to 6
- grad_out: bfloat16 [32, 1024, 4096], P('dp', 'ctx'), may hold values from -6 to 6
- doc_lengths: int32 [32, 8], P('dp'), may hold values from 1 to 512, 1024 in all within a row
- prefix_lengths: int32 [32, 8], P('dp'), may hold values from 1 to 512
- stretch_order: int32 [32, 16], P('dp'), may hold values from 0 to 15, each once within a row
Outputs:
- attn_out: bfloat16 [32, 1024, 4096], P('dp', 'ctx')
- grad_query: bfloat16 [32, 1024, 4096], P('dp', 'ctx')
- grad_key: bfloat16 [32, 1024, 512], P('dp', 'ctx')
- grad_wvalue: float32 [8192, 512], P(('dp', 'ctx'))
The draws below stay inside these ranges and needn't reach their ends.
Inputs may be any that keep to these rules, and one draw needn't show every extreme that they name: `doc_lengths`: each row sums to 1024, and its longest document has exactly 512 tokens. `prefix_lengths`: a span longer than its document covers all of it. `stretch_order`: each row names every query stretch once.
All inputs are finite; a program needn't handle non-finite values.
Results may differ from the reference program's by a relative error of at most 0.025.
Values may be sent and summed in bfloat16 or wider, within the bound.
No kernel may reach another device: no remote copies, remote signals or barrier semaphores. Data moves between devices by JAX's collectives and lax.ppermute only.
A program may use at most 128 MiB of HBM per device.

```python
import math
import jax
import jax.numpy as jnp
import numpy as np
from jax import lax

D = 8192
HEADS = 32
KV_HEADS = 4
HEAD_DIM = 128
GROUP = 8
TOK_DEV = 128
CH = 64
NDOC = 8
SEQ = 1024
SEQS = 32
NCH = 16
MAXDOC = 512
N_CTX = 8


def draw_query(key, part):
    key = jax.random.fold_in(key, 11)
    shape = (SEQS, SEQ, HEADS * HEAD_DIM)
    base = jnp.clip(jax.random.normal(key, shape, jnp.float32), -4.0, 4.0)
    return base.astype(jnp.bfloat16)


def draw_key(key, part):
    key = jax.random.fold_in(key, 23)
    shape = (SEQS, SEQ, KV_HEADS * HEAD_DIM)
    base = jnp.clip(jax.random.normal(key, shape, jnp.float32), -4.0, 4.0)
    return base.astype(jnp.bfloat16)


def touch_ends(array, key, smallest, top_value):
    dims = array.shape
    place = [jax.random.randint(jax.random.fold_in(key, axis), (), 0, dims[axis]) for axis in range(len(dims))]
    array = array.at[tuple(place)].set(smallest)
    longest = dims.index(max(dims))
    place[longest] = (place[longest] + 1) % dims[longest]
    return array.at[tuple(place)].set(top_value)


def strengthened(values, rng, source, target, shards_of, factor):
    owner, partner = [(jnp.arange(values.shape[dim]) // (values.shape[dim] // shards_of)).reshape([-1 if axis == dim else 1 for axis in range(values.ndim)]) for dim in (source, target)]
    chosen = jax.random.permutation(rng, shards_of)[partner]
    strong = (owner == chosen) | (owner == (partner + shards_of // 2) % shards_of)
    return jnp.where(strong, factor * values, values)


def levels(rng, extent, shards, smallest, largest):
    def one(axis_at, shards_of):
        draws = jax.random.uniform(jax.random.fold_in(jax.random.fold_in(rng, 6), axis_at), (shards_of,), jnp.float32, smallest / len(shards), largest / len(shards))
        return jnp.repeat(jnp.exp(draws), extent[axis_at] // shards_of).reshape((-1,) + (1,) * (len(extent) - axis_at - 1))

    loudness = one(*shards[0])
    for cut in shards[1:]:
        loudness = loudness * one(*cut)
    return loudness


def profile(number_of, total, reach, slope):
    loads = [(1 << 20) // math.isqrt(standing ** slope) + 1 for standing in range(2, number_of + 1)]
    rest, holding = total - reach - (number_of - 1), [1] * (number_of - 1)
    while rest > 0:
        candidates = [i for i in range(number_of - 1) if holding[i] < reach]
        whole, budget = sum([loads[i] for i in candidates]), rest
        for i in candidates:
            extra = min(reach - holding[i], max(1, budget * loads[i] // whole), rest)
            holding[i] = holding[i] + extra
            rest = rest - extra
    return np.array([reach] + holding)


def uneven(stream_key, amount, total, bound, slope):
    if amount == 2:
        one = jax.random.randint(stream_key, (), max(1, total - bound), min(bound, total - 1) + 1)
        return jnp.stack([one, total - one])
    sizes = jnp.asarray(profile(amount, total, bound, slope), jnp.int32)
    couples = (amount - 1) // 2
    donor, receiver = sizes[1:1 + 2 * couples:2], sizes[2:2 + 2 * couples:2]
    slack = jnp.minimum(donor - 1, bound - receiver)
    moved = jax.random.randint(jax.random.fold_in(stream_key, 1), (couples,), 0, 1 << 20) % (slack + 1)
    sizes = sizes.at[1:1 + 2 * couples:2].set(donor - moved).at[2:2 + 2 * couples:2].set(receiver + moved)
    return sizes[jax.random.permutation(jax.random.fold_in(stream_key, 2), amount)]


def noise(own_key, shape, width, limit, shards=(), kind=jnp.bfloat16):
    array = width * jax.random.normal(own_key, shape, jnp.float32)
    if shards:
        array = array * levels(own_key, shape, shards, -0.22, 0.18)
    return jnp.clip(array, -limit, limit).astype(kind)


def heavy_noise(stream_key, extent, spread, limit, pieces, heavy, held_as=jnp.bfloat16):
    values = spread * jax.random.normal(stream_key, extent, jnp.float32)
    if pieces:
        values = values * levels(stream_key, extent, pieces, -0.22, 0.18)
    return jnp.clip(strengthened(values, jax.random.fold_in(stream_key, 3), *heavy), -limit, limit).astype(held_as)


def setup_inputs(seed: int = 0) -> dict:
    arg_keys = jax.random.split(jax.random.key(seed), 9)
    return {
        "layer_input": heavy_noise(arg_keys[0], (SEQS, SEQ, D), 1.0, 6.0, ((0, 32), (1, 8)), (0, 2, 32, 2.75)),
        "query": draw_query(jax.random.fold_in(arg_keys[8], 71), 0),
        "key": draw_key(jax.random.fold_in(arg_keys[8], 71), 0),
        "value": noise(arg_keys[3], (SEQS, SEQ, KV_HEADS * HEAD_DIM), 1.0, 6.0, ((0, 32), (1, 8))),
        "grad_out": noise(arg_keys[4], (SEQS, SEQ, HEADS * HEAD_DIM), 1.0, 6.0, ((0, 32), (1, 8))),
        "doc_lengths": jax.vmap(lambda own: uneven(own, NDOC, SEQ, MAXDOC, 2))(jax.random.split(arg_keys[5], SEQS)).reshape((SEQS, NDOC)).astype(jnp.int32),
        "prefix_lengths": touch_ends(jax.random.randint(arg_keys[6], (SEQS, NDOC), 1, MAXDOC + 1), jax.random.fold_in(arg_keys[6], 1), 1, MAXDOC).astype(jnp.int32),
        "stretch_order": jax.vmap(lambda own: jax.random.permutation(own, NCH))(jax.random.split(arg_keys[7], SEQS)).reshape((SEQS, NCH)).astype(jnp.int32),
    }


neg_big = -1.0e30


def layout(order, lengths, prefix):
    within = jnp.arange(CH, dtype=jnp.int32)
    places = (order.astype(jnp.int32)[:, None] * CH + within[None, :]).reshape(-1).astype(jnp.int32)
    lengths = lengths.astype(jnp.int32)
    starts = (jnp.cumsum(lengths) - lengths).astype(jnp.int32)
    owners = (jnp.sum((starts[None, :] <= places[:, None]).astype(jnp.int32), axis=1) - 1).astype(jnp.int32)
    ends = (starts + jnp.minimum(prefix.astype(jnp.int32), lengths)).astype(jnp.int32)
    match = owners[:, None] == jnp.arange(NDOC, dtype=jnp.int32)[None, :]
    open_end = jnp.sum(jnp.where(match, ends[None, :], 0), axis=1).astype(jnp.int32)
    return places, owners, open_end


def visible(q_places, q_owners, k_places, k_owners, k_open):
    same = q_owners[:, None] == k_owners[None, :]
    seen = (k_places[None, :] <= q_places[:, None]) | (k_places[None, :] < k_open[None, :])
    return same & seen


def reference(layer_input, query, key, value, grad_out, doc_lengths, prefix_lengths, stretch_order):
    scale = HEAD_DIM ** -0.5
    kv_width = KV_HEADS * HEAD_DIM

    def one_sequence(total_weight, items):
        x_seq, q_seq, k_seq, v_seq, g_seq, lens, prefix, order = items
        places, owners, open_end = layout(order, lens, prefix)
        k3 = k_seq.reshape(SEQ, KV_HEADS, HEAD_DIM).astype(jnp.float32)
        v3 = v_seq.reshape(SEQ, KV_HEADS, HEAD_DIM).astype(jnp.float32)
        outputs = []
        query_grads = []
        key_total = jnp.zeros((SEQ, kv_width), jnp.float32)
        value_total = jnp.zeros((SEQ, kv_width), jnp.float32)
        for block in range(N_CTX):
            low = block * TOK_DEV
            high = low + TOK_DEV
            q4 = q_seq[low:high].reshape(TOK_DEV, KV_HEADS, GROUP, HEAD_DIM).astype(jnp.float32)
            g4 = g_seq[low:high].reshape(TOK_DEV, KV_HEADS, GROUP, HEAD_DIM).astype(jnp.float32)
            live = visible(places[low:high], owners[low:high], places, owners, open_end)[None, None]
            raw = jnp.einsum("qhgd,khd->hgqk", q4, k3) * scale
            masked = jnp.where(live, raw, neg_big)
            top = jnp.max(masked, axis=-1)
            mass = jnp.sum(jnp.where(live, jnp.exp(masked - top[..., None]), 0.0), axis=-1)
            lse = top + jnp.log(mass)
            probs = jnp.where(live, jnp.exp(masked - lse[..., None]), 0.0).astype(jnp.bfloat16)
            probs = lax.optimization_barrier(probs).astype(jnp.float32)
            output = jnp.einsum("hgqk,khd->qhgd", probs, v3)
            outputs.append(output.astype(jnp.bfloat16).reshape(TOK_DEV, HEADS * HEAD_DIM))
            delta = jnp.transpose(jnp.sum(g4 * output, axis=-1), (1, 2, 0))
            dots = jnp.einsum("qhgd,khd->hgqk", g4, v3)
            slopes = (probs * (dots - delta[..., None]) * scale).astype(jnp.bfloat16)
            slopes = lax.optimization_barrier(slopes).astype(jnp.float32)
            grad_q = jnp.einsum("hgqk,khd->qhgd", slopes, k3)
            query_grads.append(grad_q.astype(jnp.bfloat16).reshape(TOK_DEV, HEADS * HEAD_DIM))
            key_part = jnp.einsum("hgqk,qhgd->khd", slopes, q4).reshape(SEQ, kv_width).astype(jnp.bfloat16)
            value_part = jnp.einsum("hgqk,qhgd->khd", probs, g4).reshape(SEQ, kv_width).astype(jnp.bfloat16)
            key_part = lax.optimization_barrier(key_part)
            value_part = lax.optimization_barrier(value_part)
            key_total = key_total + key_part.astype(jnp.float32)
            value_total = value_total + value_part.astype(jnp.float32)
        grad_value = value_total.astype(jnp.bfloat16)
        for block in range(N_CTX):
            low = block * TOK_DEV
            high = low + TOK_DEV
            term = jnp.dot(x_seq[low:high].T, grad_value[low:high], preferred_element_type=jnp.float32)
            term = lax.optimization_barrier(term.astype(jnp.bfloat16))
            total_weight = total_weight + term.astype(jnp.float32)
        result = (jnp.concatenate(outputs, axis=0), jnp.concatenate(query_grads, axis=0), key_total.astype(jnp.bfloat16))
        return total_weight, result

    start = jnp.zeros((D, kv_width), jnp.float32)
    items = (layer_input, query, key, value, grad_out, doc_lengths, prefix_lengths, stretch_order)
    grad_wvalue, stacked = lax.scan(one_sequence, start, items)
    return stacked[0], stacked[1], stacked[2], grad_wvalue
```

```python
import functools
import math

import jax
import jax.numpy as jnp
from jax import lax
from jax.experimental import pallas as pl
from jax.experimental.pallas import tpu as pltpu
from jax.sharding import PartitionSpec as P

HEADS = 32
KV_HEADS = 4
HEAD_DIM = 128
GROUP = 8
CH = 64
NDOC = 8

NT = (((1,), (1,)), ((), ()))
NN = (((1,), (0,)), ((), ()))
TN = (((0,), (0,)), ((), ()))


def dot(a, b, dims):
    return lax.dot_general(a, b, dims, preferred_element_type=jnp.float32)


def fill_bias(lens, prefix, order, ctx, bias):
    rows = bias.shape[1]
    lane = lax.broadcasted_iota(jnp.int32, (8, rows), 1)
    place = lane
    for s in range(rows // CH):
        moved = order[0, ctx * (rows // CH) + s] * CH - s * CH
        place = jnp.where(lane >= s * CH, lane + moved, place)
    low = jnp.zeros((8, rows), jnp.int32)
    open_end = jnp.zeros((8, rows), jnp.int32)
    start = jnp.int32(0)
    for d in range(NDOC):
        hit = place >= start
        low = jnp.where(hit, start, low)
        open_end = jnp.where(hit, start + jnp.minimum(prefix[0, d], lens[0, d]), open_end)
        start = start + lens[0, d]
    high = jnp.maximum(place + 1, open_end)
    sub = lax.broadcasted_iota(jnp.int32, (8, rows), 0)

    def stretch(b, carry):
        base = order[0, b] * CH
        for i in range(CH // 8):
            at = sub + (base + i * 8)
            bias[pl.ds(pl.multiple_of(b * CH + i * 8, 8), 8), :] = jnp.where(
                (at >= low) & (at < high), 0.0, -1e30
            )
        return carry

    lax.fori_loop(0, bias.shape[0] // CH, stretch, 0)


def attention_kernel(lens, prefix, order, q, g, k, v, out, dq, dk, dv, bias, dk_sum, dv_sum, k_t, v_t):
    ctx = lax.axis_index("ctx")

    @pl.when(pl.program_id(0) == 0)
    def _():
        fill_bias(lens, prefix, order, ctx, bias)

    scale = HEAD_DIM**-0.5
    k_t[...] = k[...].T
    v_t[...] = v[...].T
    for c in range(GROUP // 2):
        cols = [slice((2 * c + i) * HEAD_DIM, (2 * c + i + 1) * HEAD_DIM) for i in range(2)]
        q2 = jnp.concatenate([q[:, s] for s in cols], 0)
        g2 = jnp.concatenate([g[:, s] for s in cols], 0)
        b = bias[...]
        t = dot(k[...], q2, NT) * (scale * math.log2(math.e)) + jnp.concatenate([b, b], 1)
        p = jnp.exp2(t - jnp.max(t, axis=0, keepdims=True))
        probs = (p * (1.0 / jnp.sum(p, axis=0, keepdims=True))).astype(jnp.bfloat16)
        out_t = dot(v_t[...], probs, NN)
        dots = dot(v[...], g2, NT)
        wide = probs.astype(jnp.float32)
        delta = jnp.sum(wide * dots, axis=0, keepdims=True)
        slopes = (wide * (dots - delta)).astype(jnp.bfloat16)
        dq_t = dot(k_t[...], slopes, NN) * scale
        dv_c = dot(probs, g2, NN)
        dk_c = dot(slopes, q2, NN)
        if c == 0:
            dv_sum[...] = dv_c
            dk_sum[...] = dk_c
        else:
            dv_sum[...] += dv_c
            dk_sum[...] += dk_c
        o2 = out_t.T.astype(jnp.bfloat16)
        d2 = dq_t.T.astype(jnp.bfloat16)
        for i, s in enumerate(cols):
            out[:, s] = o2[i * HEAD_DIM : (i + 1) * HEAD_DIM]
            dq[:, s] = d2[i * HEAD_DIM : (i + 1) * HEAD_DIM]
    dk[...] = (dk_sum[...] * scale).astype(jnp.bfloat16)
    dv[...] = dv_sum[...].astype(jnp.bfloat16)


def attention(q, g, both, lens, prefix, order):
    rows, total, kv_width = q.shape[0], both.shape[0], both.shape[1] // 2

    def block(r, c):
        return pl.BlockSpec((r, c), lambda h: (0, h))

    scalars = pl.BlockSpec(memory_space=pltpu.SMEM)
    wide, narrow = block(rows, GROUP * HEAD_DIM), block(total, HEAD_DIM)
    values = pl.BlockSpec((total, HEAD_DIM), lambda h: (0, h + KV_HEADS))
    shape = jax.ShapeDtypeStruct
    return pl.pallas_call(
        attention_kernel,
        grid=(KV_HEADS,),
        in_specs=[scalars] * 3 + [wide, wide, narrow, values],
        out_specs=[wide, wide, narrow, narrow],
        out_shape=[shape(q.shape, jnp.bfloat16)] * 2 + [shape((total, kv_width), jnp.bfloat16)] * 2,
        scratch_shapes=[
            pltpu.VMEM((total, rows), jnp.float32),
            pltpu.VMEM((total, HEAD_DIM), jnp.float32),
            pltpu.VMEM((total, HEAD_DIM), jnp.float32),
            pltpu.VMEM((HEAD_DIM, total), jnp.bfloat16),
            pltpu.VMEM((HEAD_DIM, total), jnp.bfloat16),
        ],
        compiler_params=pltpu.CompilerParams(vmem_limit_bytes=40 * 1024 * 1024),
        cost_estimate=pl.CostEstimate(
            flops=12 * HEADS * rows * total * HEAD_DIM, bytes_accessed=8 << 20, transcendentals=HEADS * rows * total
        ),
    )(lens, prefix, order, q, g, both, both)


def on_device(layer_input, query, key, value, grad_out, doc_lengths, prefix_lengths, stretch_order):
    both = lax.all_gather(jnp.concatenate([key[0], value[0]], 1), "ctx", axis=0, tiled=True)
    columns = lax.all_to_all(layer_input[0], "dp", split_axis=1, concat_axis=0, tiled=True)
    columns, stretch_order = lax.optimization_barrier((columns, stretch_order))
    out, dq, dk, dv = attention(query[0], grad_out[0], both, doc_lengths, prefix_lengths, stretch_order)
    dv_mine = lax.psum_scatter(dv, "ctx", scatter_dimension=0, tiled=True)
    dv_mine, dk = lax.optimization_barrier((dv_mine, dk))
    dv_batch = lax.all_gather(dv_mine, "dp", axis=0, tiled=True)
    parts = lax.all_to_all(dk, "ctx", split_axis=0, concat_axis=0, tiled=True)
    parts = parts.reshape(-1, dv_mine.shape[0], dk.shape[1]).astype(jnp.float32)
    grad_key = jnp.sum(parts, axis=0).astype(jnp.bfloat16)
    columns, grad_key = lax.optimization_barrier((columns, grad_key))
    part = dot(columns, dv_batch, TN).astype(jnp.bfloat16)
    weight = lax.psum_scatter(part, "ctx", scatter_dimension=0, tiled=True).astype(jnp.float32)
    return (out[None], dq[None], grad_key[None], weight)


def solution(mesh):
    rows = P("dp", "ctx", None)
    scalars = P("dp", None)
    return jax.shard_map(
        on_device,
        mesh=mesh,
        in_specs=(rows,) * 5 + (scalars,) * 3,
        out_specs=(rows, rows, rows, P(("dp", "ctx"), None)),
        check_vma=False,
    )
```

```python
import functools
import math

import jax
import jax.numpy as jnp
from jax import lax
from jax.experimental import pallas as pl
from jax.experimental.pallas import tpu as pltpu
from jax.sharding import PartitionSpec as P

HEADS = 32
KV_HEADS = 4
HEAD_DIM = 128
GROUP = 8
CH = 64
NDOC = 8
N_X = 4
N_Y = 4
VMEM = 56 * 1024 * 1024
DISTANCES = (0, -1, 1, -2, 2, -3, 3, 4)

NT = (((1,), (1,)), ((), ()))
NN = (((1,), (0,)), ((), ()))
TN = (((0,), (0,)), ((), ()))


def dot(a, b, dims):
    return lax.dot_general(a, b, dims, preferred_element_type=jnp.float32)


def fill_bias(lens, prefix, order, ctx, bias):
    rows = bias.shape[1]
    per = rows // CH
    n_ctx = bias.shape[0] // rows
    lane = lax.broadcasted_iota(jnp.int32, (8, rows), 1)
    place = lane
    for s in range(per):
        moved = order[0, ctx * per + s] * CH - s * CH
        place = jnp.where(lane >= s * CH, lane + moved, place)
    low = jnp.zeros((8, rows), jnp.int32)
    open_end = jnp.zeros((8, rows), jnp.int32)
    start = jnp.int32(0)
    for d in range(NDOC):
        hit = place >= start
        low = jnp.where(hit, start, low)
        open_end = jnp.where(hit, start + jnp.minimum(prefix[0, d], lens[0, d]), open_end)
        start = start + lens[0, d]
    high = jnp.maximum(place + 1, open_end)
    sub = lax.broadcasted_iota(jnp.int32, (8, rows), 0)
    for n, far in enumerate(DISTANCES):
        owner = lax.rem(ctx + far + n_ctx, n_ctx)
        for s in range(per):
            base = order[0, owner * per + s] * CH
            for i in range(CH // 8):
                at = sub + (base + i * 8)
                row = n * rows + s * CH + i * 8
                bias[row : row + 8, :] = jnp.where((at >= low) & (at < high), 0.0, -1e30)


def pair(c):
    return [slice((2 * c + i) * HEAD_DIM, (2 * c + i + 1) * HEAD_DIM) for i in range(2)]


def owners_of(n_ctx):
    ctx = lax.axis_index("ctx")
    return [lax.rem(ctx + far + n_ctx, n_ctx) for far in DISTANCES]


def probs_kernel(lens, prefix, order, q, g, *refs):
    n_ctx = len(DISTANCES)
    k_blocks = refs[:n_ctx]
    probs, dv, bias, k, total = refs[n_ctx:]
    rows = q.shape[0]

    @pl.when(pl.program_id(0) == 0)
    def _():
        fill_bias(lens, prefix, order, lax.axis_index("ctx"), bias)

    scale = HEAD_DIM**-0.5
    for n in range(n_ctx):
        k[n * rows : (n + 1) * rows] = k_blocks[n][...]
    for c in range(GROUP // 2):
        q2 = jnp.concatenate([q[:, s] for s in pair(c)], 0)
        g2 = jnp.concatenate([g[:, s] for s in pair(c)], 0)
        b = bias[...]
        t = dot(k[...], q2, NT) * (scale * math.log2(math.e)) + jnp.concatenate([b, b], 1)
        p = jnp.exp2(t - jnp.max(t, axis=0, keepdims=True))
        p = (p * (1.0 / jnp.sum(p, axis=0, keepdims=True))).astype(jnp.bfloat16)
        probs[0, :, 2 * c * HEAD_DIM : (2 * c + 2) * HEAD_DIM] = p
        dv_c = dot(p, g2, NN)
        if c == 0:
            total[...] = dv_c
        else:
            total[...] += dv_c
    for n, owner in enumerate(owners_of(n_ctx)):
        dv[owner] = total[n * rows : (n + 1) * rows].astype(jnp.bfloat16)


def grads_kernel(q, g, probs, *refs):
    n_ctx = len(DISTANCES)
    k_blocks, v_blocks = refs[:n_ctx], refs[n_ctx : 2 * n_ctx]
    out, dq, dk, v, k_t, v_t, total = refs[2 * n_ctx :]
    rows = q.shape[0]
    scale = HEAD_DIM**-0.5
    for n in range(n_ctx):
        at = slice(n * rows, (n + 1) * rows)
        v[at] = v_blocks[n][...]
        k_t[:, at] = k_blocks[n][...].T
        v_t[:, at] = v_blocks[n][...].T
    for c in range(GROUP // 2):
        q2 = jnp.concatenate([q[:, s] for s in pair(c)], 0)
        g2 = jnp.concatenate([g[:, s] for s in pair(c)], 0)
        p = probs[0, :, 2 * c * HEAD_DIM : (2 * c + 2) * HEAD_DIM]
        out_t = dot(v_t[...], p, NN)
        dots = dot(v[...], g2, NT)
        wide = p.astype(jnp.float32)
        delta = jnp.sum(wide * dots, axis=0, keepdims=True)
        slopes = (wide * (dots - delta)).astype(jnp.bfloat16)
        dq_t = dot(k_t[...], slopes, NN) * scale
        dk_c = dot(slopes, q2, NN)
        if c == 0:
            total[...] = dk_c
        else:
            total[...] += dk_c
        o2 = out_t.T.astype(jnp.bfloat16)
        d2 = dq_t.T.astype(jnp.bfloat16)
        for i, s in enumerate(pair(c)):
            out[:, s] = o2[i * HEAD_DIM : (i + 1) * HEAD_DIM]
            dq[:, s] = d2[i * HEAD_DIM : (i + 1) * HEAD_DIM]
    for n, owner in enumerate(owners_of(n_ctx)):
        dk[owner] = (total[n * rows : (n + 1) * rows] * scale).astype(jnp.bfloat16)


def specs_of(rows, n_ctx):
    wide = pl.BlockSpec((rows, GROUP * HEAD_DIM), lambda h: (0, h))
    first = pl.BlockSpec((rows, HEAD_DIM), lambda h: (0, h))
    second = pl.BlockSpec((rows, HEAD_DIM), lambda h: (0, h + KV_HEADS))
    keys, values = [first] * n_ctx, [second] * (n_ctx - 1) + [first]
    parts = pl.BlockSpec((n_ctx, rows, HEAD_DIM), lambda h: (0, 0, h))
    square = pl.BlockSpec((1, n_ctx * rows, GROUP * rows), lambda h: (h, 0, 0))
    return wide, keys, values, parts, square


def probs_and_dv(q, g, k_blocks, lens, prefix, order):
    rows, n_ctx = q.shape[0], len(k_blocks)
    kv_width, total = k_blocks[-1].shape[1], rows * n_ctx
    wide, keys, values, parts, square = specs_of(rows, n_ctx)
    shape = jax.ShapeDtypeStruct
    return pl.pallas_call(
        probs_kernel,
        grid=(KV_HEADS,),
        in_specs=[pl.BlockSpec(memory_space=pltpu.SMEM)] * 3 + [wide, wide] + keys,
        out_specs=[square, parts],
        out_shape=[
            shape((KV_HEADS, total, GROUP * rows), jnp.bfloat16),
            shape((n_ctx, rows, kv_width), jnp.bfloat16),
        ],
        scratch_shapes=[
            pltpu.VMEM((total, rows), jnp.float32),
            pltpu.VMEM((total, HEAD_DIM), jnp.bfloat16),
            pltpu.VMEM((total, HEAD_DIM), jnp.float32),
        ],
        compiler_params=pltpu.CompilerParams(vmem_limit_bytes=VMEM),
        cost_estimate=pl.CostEstimate(
            flops=4 * HEADS * rows * total * HEAD_DIM, bytes_accessed=12 << 20, transcendentals=HEADS * rows * total
        ),
    )(lens, prefix, order, q, g, *k_blocks)


def out_and_grads(q, g, probs, k_blocks, v_blocks):
    rows, n_ctx = q.shape[0], len(k_blocks)
    kv_width, total = k_blocks[-1].shape[1], rows * n_ctx
    wide, keys, values, parts, square = specs_of(rows, n_ctx)
    shape = jax.ShapeDtypeStruct
    return pl.pallas_call(
        grads_kernel,
        grid=(KV_HEADS,),
        in_specs=[wide, wide, square] + keys + values,
        out_specs=[wide, wide, parts],
        out_shape=[shape(q.shape, jnp.bfloat16)] * 2 + [shape((n_ctx, rows, kv_width), jnp.bfloat16)],
        scratch_shapes=[
            pltpu.VMEM((total, HEAD_DIM), jnp.bfloat16),
            pltpu.VMEM((HEAD_DIM, total), jnp.bfloat16),
            pltpu.VMEM((HEAD_DIM, total), jnp.bfloat16),
            pltpu.VMEM((total, HEAD_DIM), jnp.float32),
        ],
        compiler_params=pltpu.CompilerParams(vmem_limit_bytes=VMEM),
        cost_estimate=pl.CostEstimate(
            flops=8 * HEADS * rows * total * HEAD_DIM, bytes_accessed=14 << 20, transcendentals=0
        ),
    )(q, g, probs, *k_blocks, *v_blocks)


def along_ctx(a, far):
    n = lax.axis_size("ctx")
    return lax.ppermute(a, "ctx", [(i, (i + far) % n) for i in range(n)])


def place_of(i):
    return i >> 3, (i >> 1) & 3, i & 1


def index_of(y, x, core):
    return ((y % N_Y) * N_X + x % N_X) * 2 + core


def along_dp(a, dy, dx, other_core):
    pairs = []
    for i in range(lax.axis_size("dp")):
        y, x, core = place_of(i)
        pairs.append((i, index_of(y + dy, x + dx, core ^ other_core)))
    return lax.ppermute(a, "dp", pairs)


def over_x(pieces):
    return [pieces[0]] + [along_dp(pieces[d], 0, d if d < 3 else -1, 0) for d in range(1, N_X)]


def pick_kernel(where, *refs):
    half = len(refs) // 2
    for source, target in zip(refs[:half], refs[half:]):
        target[...] = source[...]


def columns_for_x(layer, y, x):
    rows, model = layer.shape
    width = model // (N_X * N_Y)

    def source(d):
        return pl.BlockSpec((rows, width), lambda j, at: (0, lax.rem(at[0] + j, N_Y) * N_X + lax.rem(at[1] + d, N_X)))

    return pl.pallas_call(
        pick_kernel,
        grid_spec=pltpu.PrefetchScalarGridSpec(
            num_scalar_prefetch=1,
            grid=(N_Y,),
            in_specs=[source(d) for d in range(N_X)],
            out_specs=[pl.BlockSpec((rows, width), lambda j, at: (0, j))] * N_X,
        ),
        out_shape=[jax.ShapeDtypeStruct((rows, model // N_X), layer.dtype)] * N_X,
        cost_estimate=pl.CostEstimate(flops=0, bytes_accessed=4 * layer.size, transcendentals=0),
    )(jnp.stack([y, x]).astype(jnp.int32), *[layer] * N_X)


def turn_kernel(where, *refs):
    mine, others = refs[2 * N_X :]
    rows = refs[0].shape[0]
    for d in range(N_X):
        at = slice(d * rows, (d + 1) * rows)
        mine[:, at] = refs[d][...].T
        others[:, at] = refs[N_X + d][...].T


def split_cores(pieces, core):
    rows, width = pieces[0].shape
    narrow = width // (2 * N_Y)
    own = pl.BlockSpec((rows, narrow), lambda j, at: (0, 2 * j + at[0]))
    other = pl.BlockSpec((rows, narrow), lambda j, at: (0, 2 * j + 1 - at[0]))
    return pl.pallas_call(
        turn_kernel,
        grid_spec=pltpu.PrefetchScalarGridSpec(
            num_scalar_prefetch=1,
            grid=(N_Y,),
            in_specs=[own] * N_X + [other] * N_X,
            out_specs=[pl.BlockSpec((narrow, N_X * rows), lambda j, at: (j, 0))] * 2,
        ),
        out_shape=[jax.ShapeDtypeStruct((width // 2, N_X * rows), pieces[0].dtype)] * 2,
        cost_estimate=pl.CostEstimate(flops=0, bytes_accessed=16 * pieces[0].size, transcendentals=0),
    )(core[None].astype(jnp.int32), *pieces, *pieces)


def on_device(layer_input, query, key, value, grad_out, doc_lengths, prefix_lengths, stretch_order):
    n_ctx = lax.axis_size("ctx")
    y, x, core = place_of(lax.axis_index("dp"))
    here = jnp.concatenate([key[0], value[0]], 1)
    half = n_ctx // 2
    width = key.shape[2]
    up, down = [here], [here]
    columns = columns_for_x(layer_input[0], y, x)
    moved = over_x(columns)
    for step in range(half - 1):
        if step == 1:
            up[1], down[1], picked = lax.optimization_barrier((up[1], down[1], columns[0]))
        up.append(along_ctx(up[-1], 1))
        down.append(along_ctx(down[-1], -1))
    far_key = along_ctx(up[-1][:, :width], 1)
    far_value = along_ctx(down[-1][:, width:], -1)
    far_key, far_value, moved[1], moved[3] = lax.optimization_barrier((far_key, far_value, moved[1], moved[3]))
    blocks = [down[far] if far > 0 else up[-far] for far in DISTANCES[:-1]]
    keys, values = blocks + [far_key], blocks + [far_value]

    q, g = query[0], grad_out[0]
    probs, dv = probs_and_dv(q, g, keys, doc_lengths, prefix_lengths, stretch_order)
    got = lax.all_to_all(dv, "ctx", split_axis=0, concat_axis=0, tiled=True)
    out, dq, dk = out_and_grads(q, g, probs, keys, values)
    moved, dk = lax.optimization_barrier(([picked] + moved[1:], dk))
    mine_t, others_t = split_cores(moved, core)
    got, mine_t, others_t = lax.optimization_barrier((got, mine_t, others_t))
    grad_value = jnp.sum(got.astype(jnp.float32), axis=0).astype(jnp.bfloat16)
    others_t = along_dp(others_t, 0, 0, 1)
    got_k = lax.all_to_all(dk, "ctx", split_axis=0, concat_axis=0, tiled=True)

    near = jnp.concatenate(over_x([grad_value] * N_X), 0)
    far = along_dp(near, 0, 0, 1)
    part = (dot(mine_t, near, NN) + dot(others_t, far, NN)).reshape(N_Y, -1, near.shape[1])
    sent = part.astype(jnp.bfloat16)
    sent, got_k = lax.optimization_barrier((sent, got_k))
    total = part[0]
    for d in range(1, N_Y):
        total = total + along_dp(sent[d], d if d < 3 else -1, 0, 0).astype(jnp.float32)
    total = total.astype(jnp.bfloat16).reshape(n_ctx, -1, near.shape[1])

    grad_key = jnp.sum(got_k.astype(jnp.float32), axis=0).astype(jnp.bfloat16)
    last = lax.all_to_all(total, "ctx", split_axis=0, concat_axis=0, tiled=True)
    weight = jnp.sum(last.astype(jnp.float32), axis=0)
    return (out[None], dq[None], grad_key[None], weight)


def solution(mesh):
    rows = P("dp", "ctx", None)
    scalars = P("dp", None)
    return jax.shard_map(
        on_device,
        mesh=mesh,
        in_specs=(rows,) * 5 + (scalars,) * 3,
        out_specs=(rows, rows, rows, P(("dp", "ctx"), None)),
        check_vma=False,
    )
```

```python
import functools
import math

import jax
import jax.numpy as jnp
from jax import lax
from jax.experimental import pallas as pl
from jax.experimental.pallas import tpu as pltpu
from jax.sharding import PartitionSpec as P

HEADS = 32
KV_HEADS = 4
HEAD_DIM = 128
GROUP = 8
CH = 64
NDOC = 8
N_X = 4
N_Y = 4
VMEM = 56 * 1024 * 1024
DISTANCES = (0, -1, 1, -2, 2, -3, 3, 4)

NT = (((1,), (1,)), ((), ()))
NN = (((1,), (0,)), ((), ()))
TN = (((0,), (0,)), ((), ()))


def dot(a, b, dims):
    return lax.dot_general(a, b, dims, preferred_element_type=jnp.float32)


def fill_bias(lens, prefix, order, ctx, bias):
    rows = bias.shape[1]
    per = rows // CH
    n_ctx = bias.shape[0] // rows
    lane = lax.broadcasted_iota(jnp.int32, (8, rows), 1)
    place = lane
    for s in range(per):
        moved = order[0, ctx * per + s] * CH - s * CH
        place = jnp.where(lane >= s * CH, lane + moved, place)
    low = jnp.zeros((8, rows), jnp.int32)
    open_end = jnp.zeros((8, rows), jnp.int32)
    start = jnp.int32(0)
    for d in range(NDOC):
        hit = place >= start
        low = jnp.where(hit, start, low)
        open_end = jnp.where(hit, start + jnp.minimum(prefix[0, d], lens[0, d]), open_end)
        start = start + lens[0, d]
    high = jnp.maximum(place + 1, open_end)
    sub = lax.broadcasted_iota(jnp.int32, (8, rows), 0)
    for n, far in enumerate(DISTANCES):
        owner = lax.rem(ctx + far + n_ctx, n_ctx)
        for s in range(per):
            base = order[0, owner * per + s] * CH
            for i in range(CH // 8):
                at = sub + (base + i * 8)
                row = n * rows + s * CH + i * 8
                bias[row : row + 8, :] = jnp.where((at >= low) & (at < high), 0.0, -1e30)


def pair(c):
    return [slice((2 * c + i) * HEAD_DIM, (2 * c + i + 1) * HEAD_DIM) for i in range(2)]


def owners_of(n_ctx):
    ctx = lax.axis_index("ctx")
    return [lax.rem(ctx + far + n_ctx, n_ctx) for far in DISTANCES]


def probs_kernel(lens, prefix, order, q, g, *refs):
    n_ctx = len(DISTANCES)
    k_blocks = refs[:n_ctx]
    probs, dv, bias, k, total = refs[n_ctx:]
    rows = q.shape[0]

    @pl.when(pl.program_id(0) == 0)
    def _():
        fill_bias(lens, prefix, order, lax.axis_index("ctx"), bias)

    scale = HEAD_DIM**-0.5
    for n in range(n_ctx):
        k[n * rows : (n + 1) * rows] = k_blocks[n][...]
    for c in range(GROUP // 2):
        q2 = jnp.concatenate([q[:, s] for s in pair(c)], 0)
        g2 = jnp.concatenate([g[:, s] for s in pair(c)], 0)
        b = bias[...]
        t = dot(k[...], q2, NT) * (scale * math.log2(math.e)) + jnp.concatenate([b, b], 1)
        p = jnp.exp2(t - jnp.max(t, axis=0, keepdims=True))
        p = (p * (1.0 / jnp.sum(p, axis=0, keepdims=True))).astype(jnp.bfloat16)
        probs[0, :, 2 * c * HEAD_DIM : (2 * c + 2) * HEAD_DIM] = p
        dv_c = dot(p, g2, NN)
        if c == 0:
            total[...] = dv_c
        else:
            total[...] += dv_c
    for n, owner in enumerate(owners_of(n_ctx)):
        dv[owner] = total[n * rows : (n + 1) * rows].astype(jnp.bfloat16)


def grads_kernel(q, g, probs, *refs):
    n_ctx = len(DISTANCES)
    k_blocks, v_blocks = refs[:n_ctx], refs[n_ctx : 2 * n_ctx]
    out, dq = refs[2 * n_ctx : 2 * n_ctx + 2]
    dk, (v, k_t, v_t, total) = refs[2 * n_ctx + 2 : 3 * n_ctx + 2], refs[3 * n_ctx + 2 :]
    rows = q.shape[0]
    scale = HEAD_DIM**-0.5
    for n in range(n_ctx):
        at = slice(n * rows, (n + 1) * rows)
        v[at] = v_blocks[n][...]
        k_t[:, at] = k_blocks[n][...].T
        v_t[:, at] = v_blocks[n][...].T
    for c in range(GROUP // 2):
        q2 = jnp.concatenate([q[:, s] for s in pair(c)], 0)
        g2 = jnp.concatenate([g[:, s] for s in pair(c)], 0)
        p = probs[0, :, 2 * c * HEAD_DIM : (2 * c + 2) * HEAD_DIM]
        out_t = dot(v_t[...], p, NN)
        dots = dot(v[...], g2, NT)
        wide = p.astype(jnp.float32)
        delta = jnp.sum(wide * dots, axis=0, keepdims=True)
        slopes = (wide * (dots - delta)).astype(jnp.bfloat16)
        dq_t = dot(k_t[...], slopes, NN) * scale
        dk_c = dot(slopes, q2, NN)
        if c == 0:
            total[...] = dk_c
        else:
            total[...] += dk_c
        o2 = out_t.T.astype(jnp.bfloat16)
        d2 = dq_t.T.astype(jnp.bfloat16)
        for i, s in enumerate(pair(c)):
            out[:, s] = o2[i * HEAD_DIM : (i + 1) * HEAD_DIM]
            dq[:, s] = d2[i * HEAD_DIM : (i + 1) * HEAD_DIM]
    for n in range(n_ctx):
        dk[n][...] = (total[n * rows : (n + 1) * rows] * scale).astype(jnp.bfloat16)


def specs_of(rows, n_ctx):
    wide = pl.BlockSpec((rows, GROUP * HEAD_DIM), lambda h: (0, h))
    first = pl.BlockSpec((rows, HEAD_DIM), lambda h: (0, h))
    second = pl.BlockSpec((rows, HEAD_DIM), lambda h: (0, h + KV_HEADS))
    keys, values = [first] * n_ctx, [second] * (n_ctx - 1) + [first]
    parts = pl.BlockSpec((n_ctx, rows, HEAD_DIM), lambda h: (0, 0, h))
    square = pl.BlockSpec((1, n_ctx * rows, GROUP * rows), lambda h: (h, 0, 0))
    return wide, keys, values, parts, square


def probs_and_dv(q, g, k_blocks, lens, prefix, order):
    rows, n_ctx = q.shape[0], len(k_blocks)
    kv_width, total = k_blocks[-1].shape[1], rows * n_ctx
    wide, keys, values, parts, square = specs_of(rows, n_ctx)
    shape = jax.ShapeDtypeStruct
    return pl.pallas_call(
        probs_kernel,
        grid=(KV_HEADS,),
        in_specs=[pl.BlockSpec(memory_space=pltpu.SMEM)] * 3 + [wide, wide] + keys,
        out_specs=[square, parts],
        out_shape=[
            shape((KV_HEADS, total, GROUP * rows), jnp.bfloat16),
            shape((n_ctx, rows, kv_width), jnp.bfloat16),
        ],
        scratch_shapes=[
            pltpu.VMEM((total, rows), jnp.float32),
            pltpu.VMEM((total, HEAD_DIM), jnp.bfloat16),
            pltpu.VMEM((total, HEAD_DIM), jnp.float32),
        ],
        compiler_params=pltpu.CompilerParams(vmem_limit_bytes=VMEM),
        cost_estimate=pl.CostEstimate(
            flops=4 * HEADS * rows * total * HEAD_DIM, bytes_accessed=12 << 20, transcendentals=HEADS * rows * total
        ),
    )(lens, prefix, order, q, g, *k_blocks)


def out_and_grads(q, g, probs, k_blocks, v_blocks):
    rows, n_ctx = q.shape[0], len(k_blocks)
    kv_width, total = k_blocks[-1].shape[1], rows * n_ctx
    wide, keys, values, parts, square = specs_of(rows, n_ctx)
    shape = jax.ShapeDtypeStruct
    return pl.pallas_call(
        grads_kernel,
        grid=(KV_HEADS,),
        in_specs=[wide, wide, square] + keys + values,
        out_specs=[wide, wide] + [keys[0]] * n_ctx,
        out_shape=[shape(q.shape, jnp.bfloat16)] * 2 + [shape((rows, kv_width), jnp.bfloat16)] * n_ctx,
        scratch_shapes=[
            pltpu.VMEM((total, HEAD_DIM), jnp.bfloat16),
            pltpu.VMEM((HEAD_DIM, total), jnp.bfloat16),
            pltpu.VMEM((HEAD_DIM, total), jnp.bfloat16),
            pltpu.VMEM((total, HEAD_DIM), jnp.float32),
        ],
        compiler_params=pltpu.CompilerParams(vmem_limit_bytes=VMEM),
        cost_estimate=pl.CostEstimate(
            flops=8 * HEADS * rows * total * HEAD_DIM, bytes_accessed=14 << 20, transcendentals=0
        ),
    )(q, g, probs, *k_blocks, *v_blocks)


def along_ctx(a, far):
    n = lax.axis_size("ctx")
    return lax.ppermute(a, "ctx", [(i, (i + far) % n) for i in range(n)])


def plus(a, b):
    return (a.astype(jnp.float32) + b.astype(jnp.float32)).astype(jnp.bfloat16)


def place_of(i):
    return i >> 3, (i >> 1) & 3, i & 1


def index_of(y, x, core):
    return ((y % N_Y) * N_X + x % N_X) * 2 + core


def along_dp(a, dy, dx, other_core):
    pairs = []
    for i in range(lax.axis_size("dp")):
        y, x, core = place_of(i)
        pairs.append((i, index_of(y + dy, x + dx, core ^ other_core)))
    return lax.ppermute(a, "dp", pairs)


def over_x(pieces):
    return [pieces[0]] + [along_dp(pieces[d], 0, d if d < 3 else -1, 0) for d in range(1, N_X)]


def turn_kernel(where, *refs):
    targets = refs[2 * N_X :]
    for d in range(N_X):
        targets[d][0] = refs[d][...].T
        targets[d][1] = refs[N_X + d][...].T


def columns_for_x(layer, y, x, core):
    rows, model = layer.shape
    width = model // (N_X * N_Y * 2)

    def place(j, at, d):
        return (lax.rem(at[0] + j, N_Y) * N_X + lax.rem(at[1] + d, N_X)) * 2

    def mine(d):
        return pl.BlockSpec((rows, width), lambda j, at: (0, place(j, at, d) + at[2]))

    def other(d):
        return pl.BlockSpec((rows, width), lambda j, at: (0, place(j, at, d) + 1 - at[2]))

    return pl.pallas_call(
        turn_kernel,
        grid_spec=pltpu.PrefetchScalarGridSpec(
            num_scalar_prefetch=1,
            grid=(N_Y,),
            in_specs=[mine(d) for d in range(N_X)] + [other(d) for d in range(N_X)],
            out_specs=[pl.BlockSpec((2, width, rows), lambda j, at: (0, j, 0))] * N_X,
        ),
        out_shape=[jax.ShapeDtypeStruct((2, N_Y * width, rows), layer.dtype)] * N_X,
        cost_estimate=pl.CostEstimate(flops=0, bytes_accessed=4 * layer.size, transcendentals=0),
    )(jnp.stack([y, x, core]).astype(jnp.int32), *[layer] * (2 * N_X))


def weight_kernel(*refs):
    columns, (others, last_others, near, far, own), sent = refs[:N_X], refs[N_X : N_X + 5], refs[N_X + 5 :]
    rows = own.shape[0]
    tokens = near.shape[0] // N_X
    both = [
        jnp.concatenate([near[d * tokens : (d + 1) * tokens], far[d * tokens : (d + 1) * tokens]], 0) for d in range(N_X)
    ]
    for j in range(N_Y):
        at = slice(j * rows, (j + 1) * rows)
        away = [others[0, at], others[1, at], last_others[at], others[2, at]]
        pairs = [jnp.concatenate([columns[d][0, at], away[d]], 1) for d in range(N_X)]
        term = sum(dot(pairs[d], both[d], NN) for d in range(N_X))
        if j == 0:
            own[...] = term
        else:
            sent[j - 1][...] = term.astype(jnp.bfloat16)


def weight_terms(columns, others, last_others, near, far):
    rows, width = columns[0].shape[1] // N_Y, near.shape[1]
    shape = jax.ShapeDtypeStruct
    halves = pl.BlockSpec((1,) + columns[0].shape[1:], lambda i: (0, 0, 0))
    whole = [pl.BlockSpec(a.shape, lambda i, n=a.ndim: (0,) * n) for a in (others, last_others, near, far)]
    part = pl.BlockSpec((rows, width), lambda i: (0, 0))
    own, *sent = pl.pallas_call(
        weight_kernel,
        grid=(1,),
        in_specs=[halves] * N_X + whole,
        out_specs=[part] * N_Y,
        out_shape=[shape((rows, width), jnp.float32)] + [shape((rows, width), jnp.bfloat16)] * (N_Y - 1),
        compiler_params=pltpu.CompilerParams(vmem_limit_bytes=VMEM // 4),
        cost_estimate=pl.CostEstimate(flops=0, bytes_accessed=1 << 16, transcendentals=0),
    )(*columns, others, last_others, near, far)
    return own, sent


def on_device(layer_input, query, key, value, grad_out, doc_lengths, prefix_lengths, stretch_order):
    n_ctx = lax.axis_size("ctx")
    y, x, core = place_of(lax.axis_index("dp"))
    here = jnp.concatenate([key[0], value[0]], 1)
    half = n_ctx // 2
    width = key.shape[2]
    up, down = [here], [here]
    columns = columns_for_x(layer_input[0], y, x, core)
    moved = over_x(columns)
    for step in range(half - 1):
        if step == 1:
            up[1], down[1], picked = lax.optimization_barrier((up[1], down[1], columns[0]))
        up.append(along_ctx(up[-1], 1))
        down.append(along_ctx(down[-1], -1))
    far_key = along_ctx(up[-1][:, :width], 1)
    far_value = along_ctx(down[-1][:, width:], -1)
    far_key, far_value, moved[1], moved[3] = lax.optimization_barrier((far_key, far_value, moved[1], moved[3]))
    blocks = [down[far] if far > 0 else up[-far] for far in DISTANCES[:-1]]
    keys, values = blocks + [far_key], blocks + [far_value]

    q, g = query[0], grad_out[0]
    probs, dv = probs_and_dv(q, g, keys, doc_lengths, prefix_lengths, stretch_order)
    got = lax.all_to_all(dv, "ctx", split_axis=0, concat_axis=0, tiled=True)
    moved[0] = picked
    early = jnp.stack([moved[d][1] for d in (0, 1, 3)])
    probs, early = lax.optimization_barrier((probs, early))
    others = along_dp(early, 0, 0, 1)
    out, dq, *parts = out_and_grads(q, g, probs, keys, values)
    parts = dict(zip(DISTANCES, parts))
    moved[2], parts[half] = lax.optimization_barrier((moved[2], parts[half]))
    last_others = along_dp(moved[2][1], 0, 0, 1)

    rising, falling = along_ctx(parts[half], 1), along_ctx(parts[1 - half], -1)
    got, rising, falling = lax.optimization_barrier((got, rising, falling))
    grad_value = jnp.sum(got.astype(jnp.float32), axis=0).astype(jnp.bfloat16)
    rising, falling = plus(rising, parts[half - 1]), plus(falling, parts[2 - half])
    rising, falling = along_ctx(rising, 1), along_ctx(falling, -1)

    near = jnp.concatenate(over_x([grad_value] * N_X), 0)
    near, rising, falling = lax.optimization_barrier((near, rising, falling))
    far = along_dp(near, 0, 0, 1)
    rising, falling = plus(rising, parts[half - 2]), plus(falling, parts[3 - half])
    rising, falling = along_ctx(rising, 1), along_ctx(falling, -1)
    own, sent = weight_terms(moved, others, last_others, near, far)
    total = own
    for d in range(1, N_Y):
        total = total + along_dp(sent[d - 1], d if d < 3 else -1, 0, 0).astype(jnp.float32)
    total = total.astype(jnp.bfloat16).reshape(n_ctx, -1, near.shape[1])
    total, rising, falling = lax.optimization_barrier((total, rising, falling))
    rising = along_ctx(plus(rising, parts[half - 3]), 1)

    grad_key = plus(plus(rising, falling), parts[0])
    last = lax.all_to_all(total, "ctx", split_axis=0, concat_axis=0, tiled=True)
    weight = jnp.sum(last.astype(jnp.float32), axis=0)
    return (out[None], dq[None], grad_key[None], weight)


def solution(mesh):
    rows = P("dp", "ctx", None)
    scalars = P("dp", None)
    return jax.shard_map(
        on_device,
        mesh=mesh,
        in_specs=(rows,) * 5 + (scalars,) * 3,
        out_specs=(rows, rows, rows, P(("dp", "ctx"), None)),
        check_vma=False,
    )
```

```python
import functools
import math

import jax
import jax.numpy as jnp
from jax import lax
from jax.experimental import pallas as pl
from jax.experimental.pallas import tpu as pltpu
from jax.sharding import PartitionSpec as P

HEADS = 32
KV_HEADS = 4
HEAD_DIM = 128
GROUP = 8
CH = 64
NDOC = 8
N_X = 4
N_Y = 4
VMEM = 56 * 1024 * 1024
DISTANCES = (0, -1, 1, -2, 2, -3, 3, 4)

NT = (((1,), (1,)), ((), ()))
NN = (((1,), (0,)), ((), ()))
TN = (((0,), (0,)), ((), ()))


def dot(a, b, dims):
    return lax.dot_general(a, b, dims, preferred_element_type=jnp.float32)


def fill_bias(lens, prefix, order, ctx, bias):
    rows = bias.shape[1]
    per = rows // CH
    n_ctx = bias.shape[0] // rows
    lane = lax.broadcasted_iota(jnp.int32, (8, rows), 1)
    place = lane
    for s in range(per):
        moved = order[0, ctx * per + s] * CH - s * CH
        place = jnp.where(lane >= s * CH, lane + moved, place)
    low = jnp.zeros((8, rows), jnp.int32)
    open_end = jnp.zeros((8, rows), jnp.int32)
    start = jnp.int32(0)
    for d in range(NDOC):
        hit = place >= start
        low = jnp.where(hit, start, low)
        open_end = jnp.where(hit, start + jnp.minimum(prefix[0, d], lens[0, d]), open_end)
        start = start + lens[0, d]
    high = jnp.maximum(place + 1, open_end)
    sub = lax.broadcasted_iota(jnp.int32, (8, rows), 0)
    for n, far in enumerate(DISTANCES):
        owner = lax.rem(ctx + far + n_ctx, n_ctx)
        for s in range(per):
            base = order[0, owner * per + s] * CH
            for i in range(CH // 8):
                at = sub + (base + i * 8)
                row = n * rows + s * CH + i * 8
                bias[row : row + 8, :] = jnp.where((at >= low) & (at < high), 0.0, -1e30)


def pair(c):
    return [slice((2 * c + i) * HEAD_DIM, (2 * c + i + 1) * HEAD_DIM) for i in range(2)]


def owners_of(n_ctx):
    ctx = lax.axis_index("ctx")
    return [lax.rem(ctx + far + n_ctx, n_ctx) for far in DISTANCES]


def probs_kernel(lens, prefix, order, q, g, *refs):
    n_ctx = len(DISTANCES)
    k_blocks = refs[:n_ctx]
    probs, dv, bias, k, total = refs[n_ctx:]
    rows = q.shape[0]

    @pl.when(pl.program_id(0) == 0)
    def _():
        fill_bias(lens, prefix, order, lax.axis_index("ctx"), bias)

    scale = HEAD_DIM**-0.5
    for n in range(n_ctx):
        k[n * rows : (n + 1) * rows] = k_blocks[n][...]
    for c in range(GROUP // 2):
        q2 = jnp.concatenate([q[:, s] for s in pair(c)], 0)
        g2 = jnp.concatenate([g[:, s] for s in pair(c)], 0)
        b = bias[...]
        t = dot(k[...], q2, NT) * (scale * math.log2(math.e)) + jnp.concatenate([b, b], 1)
        p = jnp.exp2(t - jnp.max(t, axis=0, keepdims=True))
        p = (p * (1.0 / jnp.sum(p, axis=0, keepdims=True))).astype(jnp.bfloat16)
        probs[0, :, 2 * c * HEAD_DIM : (2 * c + 2) * HEAD_DIM] = p
        dv_c = dot(p, g2, NN)
        if c == 0:
            total[...] = dv_c
        else:
            total[...] += dv_c
    for n, owner in enumerate(owners_of(n_ctx)):
        dv[owner] = total[n * rows : (n + 1) * rows].astype(jnp.bfloat16)


def grads_kernel(q, g, probs, *refs):
    n_ctx = len(DISTANCES)
    k_blocks, v_blocks = refs[:n_ctx], refs[n_ctx : 2 * n_ctx]
    out, dq = refs[2 * n_ctx : 2 * n_ctx + 2]
    dk, (v, k_t, v_t, total) = refs[2 * n_ctx + 2 : 3 * n_ctx + 2], refs[3 * n_ctx + 2 :]
    rows = q.shape[0]
    scale = HEAD_DIM**-0.5
    for n in range(n_ctx):
        at = slice(n * rows, (n + 1) * rows)
        v[at] = v_blocks[n][...]
        k_t[:, at] = k_blocks[n][...].T
        v_t[:, at] = v_blocks[n][...].T
    for c in range(GROUP // 2):
        q2 = jnp.concatenate([q[:, s] for s in pair(c)], 0)
        g2 = jnp.concatenate([g[:, s] for s in pair(c)], 0)
        p = probs[0, :, 2 * c * HEAD_DIM : (2 * c + 2) * HEAD_DIM]
        out_t = dot(v_t[...], p, NN)
        g_t = g2.T
        delta = jnp.sum(g_t.astype(jnp.float32) * out_t, axis=0, keepdims=True)
        dots = dot(v[...], g_t, NN)
        slopes = (p.astype(jnp.float32) * (dots - delta)).astype(jnp.bfloat16)
        dq_t = dot(k_t[...], slopes, NN) * scale
        dk_c = dot(slopes, q2, NN)
        if c == 0:
            total[...] = dk_c
        else:
            total[...] += dk_c
        o2 = out_t.T.astype(jnp.bfloat16)
        d2 = dq_t.T.astype(jnp.bfloat16)
        for i, s in enumerate(pair(c)):
            out[:, s] = o2[i * HEAD_DIM : (i + 1) * HEAD_DIM]
            dq[:, s] = d2[i * HEAD_DIM : (i + 1) * HEAD_DIM]
    for n in range(n_ctx):
        dk[n][...] = (total[n * rows : (n + 1) * rows] * scale).astype(jnp.bfloat16)


def specs_of(rows, n_ctx):
    wide = pl.BlockSpec((rows, GROUP * HEAD_DIM), lambda h: (0, h))
    first = pl.BlockSpec((rows, HEAD_DIM), lambda h: (0, h))
    second = pl.BlockSpec((rows, HEAD_DIM), lambda h: (0, h + KV_HEADS))
    keys, values = [first] * n_ctx, [second] * (n_ctx - 1) + [first]
    parts = pl.BlockSpec((n_ctx, rows, HEAD_DIM), lambda h: (0, 0, h))
    square = pl.BlockSpec((1, n_ctx * rows, GROUP * rows), lambda h: (h, 0, 0))
    return wide, keys, values, parts, square


def probs_and_dv(q, g, k_blocks, lens, prefix, order):
    rows, n_ctx = q.shape[0], len(k_blocks)
    kv_width, total = k_blocks[-1].shape[1], rows * n_ctx
    wide, keys, values, parts, square = specs_of(rows, n_ctx)
    shape = jax.ShapeDtypeStruct
    return pl.pallas_call(
        probs_kernel,
        grid=(KV_HEADS,),
        in_specs=[pl.BlockSpec(memory_space=pltpu.SMEM)] * 3 + [wide, wide] + keys,
        out_specs=[square, parts],
        out_shape=[
            shape((KV_HEADS, total, GROUP * rows), jnp.bfloat16),
            shape((n_ctx, rows, kv_width), jnp.bfloat16),
        ],
        scratch_shapes=[
            pltpu.VMEM((total, rows), jnp.float32),
            pltpu.VMEM((total, HEAD_DIM), jnp.bfloat16),
            pltpu.VMEM((total, HEAD_DIM), jnp.float32),
        ],
        compiler_params=pltpu.CompilerParams(vmem_limit_bytes=VMEM),
        cost_estimate=pl.CostEstimate(
            flops=4 * HEADS * rows * total * HEAD_DIM, bytes_accessed=12 << 20, transcendentals=HEADS * rows * total
        ),
    )(lens, prefix, order, q, g, *k_blocks)


def out_and_grads(q, g, probs, k_blocks, v_blocks):
    rows, n_ctx = q.shape[0], len(k_blocks)
    kv_width, total = k_blocks[-1].shape[1], rows * n_ctx
    wide, keys, values, parts, square = specs_of(rows, n_ctx)
    shape = jax.ShapeDtypeStruct
    return pl.pallas_call(
        grads_kernel,
        grid=(KV_HEADS,),
        in_specs=[wide, wide, square] + keys + values,
        out_specs=[wide, wide] + [keys[0]] * n_ctx,
        out_shape=[shape(q.shape, jnp.bfloat16)] * 2 + [shape((rows, kv_width), jnp.bfloat16)] * n_ctx,
        scratch_shapes=[
            pltpu.VMEM((total, HEAD_DIM), jnp.bfloat16),
            pltpu.VMEM((HEAD_DIM, total), jnp.bfloat16),
            pltpu.VMEM((HEAD_DIM, total), jnp.bfloat16),
            pltpu.VMEM((total, HEAD_DIM), jnp.float32),
        ],
        compiler_params=pltpu.CompilerParams(vmem_limit_bytes=VMEM),
        cost_estimate=pl.CostEstimate(
            flops=8 * HEADS * rows * total * HEAD_DIM, bytes_accessed=14 << 20, transcendentals=0
        ),
    )(q, g, probs, *k_blocks, *v_blocks)


def along_ctx(a, far):
    n = lax.axis_size("ctx")
    return lax.ppermute(a, "ctx", [(i, (i + far) % n) for i in range(n)])


def plus(a, b):
    return (a.astype(jnp.float32) + b.astype(jnp.float32)).astype(jnp.bfloat16)


def place_of(i):
    return i >> 3, (i >> 1) & 3, i & 1


def index_of(y, x, core):
    return ((y % N_Y) * N_X + x % N_X) * 2 + core


def along_dp(a, dy, dx, other_core):
    pairs = []
    for i in range(lax.axis_size("dp")):
        y, x, core = place_of(i)
        pairs.append((i, index_of(y + dy, x + dx, core ^ other_core)))
    return lax.ppermute(a, "dp", pairs)


def over_x(pieces):
    return [pieces[0]] + [along_dp(pieces[d], 0, d if d < 3 else -1, 0) for d in range(1, N_X)]


def turn_kernel(where, *refs):
    targets = refs[2 * N_X :]
    for d in range(N_X):
        targets[d][0] = refs[d][...].T
        targets[d][1] = refs[N_X + d][...].T


def columns_for_x(layer, y, x, core):
    rows, model = layer.shape
    width = model // (N_X * N_Y * 2)

    def place(j, at, d):
        return (lax.rem(at[0] + j, N_Y) * N_X + lax.rem(at[1] + d, N_X)) * 2

    def mine(d):
        return pl.BlockSpec((rows, width), lambda j, at: (0, place(j, at, d) + at[2]))

    def other(d):
        return pl.BlockSpec((rows, width), lambda j, at: (0, place(j, at, d) + 1 - at[2]))

    return pl.pallas_call(
        turn_kernel,
        grid_spec=pltpu.PrefetchScalarGridSpec(
            num_scalar_prefetch=1,
            grid=(N_Y,),
            in_specs=[mine(d) for d in range(N_X)] + [other(d) for d in range(N_X)],
            out_specs=[pl.BlockSpec((2, width, rows), lambda j, at: (0, j, 0))] * N_X,
        ),
        out_shape=[jax.ShapeDtypeStruct((2, N_Y * width, rows), layer.dtype)] * N_X,
        cost_estimate=pl.CostEstimate(flops=0, bytes_accessed=4 * layer.size, transcendentals=0),
    )(jnp.stack([y, x, core]).astype(jnp.int32), *[layer] * (2 * N_X))


def weight_kernel(*refs):
    columns, (others, last_others, near, far, own), sent = refs[:N_X], refs[N_X : N_X + 5], refs[N_X + 5 :]
    rows = own.shape[0]
    tokens = near.shape[0] // N_X
    both = [
        jnp.concatenate([near[d * tokens : (d + 1) * tokens], far[d * tokens : (d + 1) * tokens]], 0) for d in range(N_X)
    ]
    for j in range(N_Y):
        at = slice(j * rows, (j + 1) * rows)
        away = [others[0, at], others[1, at], last_others[at], others[2, at]]
        pairs = [jnp.concatenate([columns[d][0, at], away[d]], 1) for d in range(N_X)]
        term = sum(dot(pairs[d], both[d], NN) for d in range(N_X))
        if j == 0:
            own[...] = term
        else:
            sent[j - 1][...] = term.astype(jnp.bfloat16)


def weight_terms(columns, others, last_others, near, far):
    rows, width = columns[0].shape[1] // N_Y, near.shape[1]
    shape = jax.ShapeDtypeStruct
    halves = pl.BlockSpec((1,) + columns[0].shape[1:], lambda i: (0, 0, 0))
    whole = [pl.BlockSpec(a.shape, lambda i, n=a.ndim: (0,) * n) for a in (others, last_others, near, far)]
    part = pl.BlockSpec((rows, width), lambda i: (0, 0))
    own, *sent = pl.pallas_call(
        weight_kernel,
        grid=(1,),
        in_specs=[halves] * N_X + whole,
        out_specs=[part] * N_Y,
        out_shape=[shape((rows, width), jnp.float32)] + [shape((rows, width), jnp.bfloat16)] * (N_Y - 1),
        compiler_params=pltpu.CompilerParams(vmem_limit_bytes=VMEM // 4),
        cost_estimate=pl.CostEstimate(flops=0, bytes_accessed=1 << 16, transcendentals=0),
    )(*columns, others, last_others, near, far)
    return own, sent


def on_device(layer_input, query, key, value, grad_out, doc_lengths, prefix_lengths, stretch_order):
    n_ctx = lax.axis_size("ctx")
    y, x, core = place_of(lax.axis_index("dp"))
    here = jnp.concatenate([key[0], value[0]], 1)
    half = n_ctx // 2
    width = key.shape[2]
    up, down = [here], [here]
    columns = columns_for_x(layer_input[0], y, x, core)
    moved = over_x(columns)
    for step in range(half - 1):
        if step == 1:
            up[1], down[1], picked = lax.optimization_barrier((up[1], down[1], columns[0]))
        up.append(along_ctx(up[-1], 1))
        down.append(along_ctx(down[-1], -1))
    far_key = along_ctx(up[-1][:, :width], 1)
    far_value = along_ctx(down[-1][:, width:], -1)
    far_key, far_value, moved[1], moved[3] = lax.optimization_barrier((far_key, far_value, moved[1], moved[3]))
    blocks = [down[far] if far > 0 else up[-far] for far in DISTANCES[:-1]]
    keys, values = blocks + [far_key], blocks + [far_value]

    q, g = query[0], grad_out[0]
    probs, dv = probs_and_dv(q, g, keys, doc_lengths, prefix_lengths, stretch_order)
    got = lax.all_to_all(dv, "ctx", split_axis=0, concat_axis=0, tiled=True)
    moved[0] = picked
    early = jnp.stack([moved[d][1] for d in (0, 1, 3)])
    probs, early = lax.optimization_barrier((probs, early))
    others = along_dp(early, 0, 0, 1)
    out, dq, *parts = out_and_grads(q, g, probs, keys, values)
    parts = dict(zip(DISTANCES, parts))
    moved[2], parts[half] = lax.optimization_barrier((moved[2], parts[half]))
    last_others = along_dp(moved[2][1], 0, 0, 1)

    rising, falling = along_ctx(parts[half], 1), along_ctx(parts[1 - half], -1)
    got, rising, falling = lax.optimization_barrier((got, rising, falling))
    grad_value = jnp.sum(got.astype(jnp.float32), axis=0).astype(jnp.bfloat16)
    rising, falling = plus(rising, parts[half - 1]), plus(falling, parts[2 - half])
    rising, falling = along_ctx(rising, 1), along_ctx(falling, -1)

    near = jnp.concatenate(over_x([grad_value] * N_X), 0)
    near, rising, falling = lax.optimization_barrier((near, rising, falling))
    far = along_dp(near, 0, 0, 1)
    rising, falling = plus(rising, parts[half - 2]), plus(falling, parts[3 - half])
    rising, falling = along_ctx(rising, 1), along_ctx(falling, -1)
    own, sent = weight_terms(moved, others, last_others, near, far)
    total = own
    for d in range(1, N_Y):
        total = total + along_dp(sent[d - 1], d if d < 3 else -1, 0, 0).astype(jnp.float32)
    total = total.astype(jnp.bfloat16).reshape(n_ctx, -1, near.shape[1])
    total, rising, falling = lax.optimization_barrier((total, rising, falling))
    rising = along_ctx(plus(rising, parts[half - 3]), 1)

    grad_key = plus(plus(rising, falling), parts[0])
    last = lax.all_to_all(total, "ctx", split_axis=0, concat_axis=0, tiled=True)
    weight = jnp.sum(last.astype(jnp.float32), axis=0)
    return (out[None], dq[None], grad_key[None], weight)


def solution(mesh):
    rows = P("dp", "ctx", None)
    scalars = P("dp", None)
    return jax.shard_map(
        on_device,
        mesh=mesh,
        in_specs=(rows,) * 5 + (scalars,) * 3,
        out_specs=(rows, rows, rows, P(("dp", "ctx"), None)),
        check_vma=False,
    )
```

```python
import functools
import math

import jax
import jax.numpy as jnp
from jax import lax
from jax.experimental import pallas as pl
from jax.experimental.pallas import tpu as pltpu
from jax.sharding import PartitionSpec as P

HEADS = 32
KV_HEADS = 4
HEAD_DIM = 128
GROUP = 8
CH = 64
NDOC = 8
N_X = 4
N_Y = 4
VMEM = 56 * 1024 * 1024
DISTANCES = (0, -1, 1, -2, 2, -3, 3, 4)

NT = (((1,), (1,)), ((), ()))
NN = (((1,), (0,)), ((), ()))
TN = (((0,), (0,)), ((), ()))


def dot(a, b, dims):
    return lax.dot_general(a, b, dims, preferred_element_type=jnp.float32)


def fill_bias(lens, prefix, order, ctx, bias):
    rows = bias.shape[1]
    per = rows // CH
    n_ctx = bias.shape[0] // rows
    lane = lax.broadcasted_iota(jnp.int32, (8, rows), 1)
    place = lane
    for s in range(per):
        moved = order[0, ctx * per + s] * CH - s * CH
        place = jnp.where(lane >= s * CH, lane + moved, place)
    low = jnp.zeros((8, rows), jnp.int32)
    open_end = jnp.zeros((8, rows), jnp.int32)
    start = jnp.int32(0)
    for d in range(NDOC):
        hit = place >= start
        low = jnp.where(hit, start, low)
        open_end = jnp.where(hit, start + jnp.minimum(prefix[0, d], lens[0, d]), open_end)
        start = start + lens[0, d]
    high = jnp.maximum(place + 1, open_end)
    sub = lax.broadcasted_iota(jnp.int32, (8, rows), 0)
    for n, far in enumerate(DISTANCES):
        owner = lax.rem(ctx + far + n_ctx, n_ctx)
        for s in range(per):
            base = order[0, owner * per + s] * CH
            for i in range(CH // 8):
                at = sub + (base + i * 8)
                row = n * rows + s * CH + i * 8
                bias[row : row + 8, :] = jnp.where((at >= low) & (at < high), 0.0, -1e30)


def pair(c):
    return [slice((2 * c + i) * HEAD_DIM, (2 * c + i + 1) * HEAD_DIM) for i in range(2)]


def owners_of(n_ctx):
    ctx = lax.axis_index("ctx")
    return [lax.rem(ctx + far + n_ctx, n_ctx) for far in DISTANCES]


def probs_kernel(lens, prefix, order, q, g, *refs):
    n_ctx = len(DISTANCES)
    k_blocks = refs[:n_ctx]
    probs, dv, bias, k, total = refs[n_ctx:]
    rows = q.shape[0]

    @pl.when(pl.program_id(0) == 0)
    def _():
        fill_bias(lens, prefix, order, lax.axis_index("ctx"), bias)

    scale = HEAD_DIM**-0.5
    for n in range(n_ctx):
        k[n * rows : (n + 1) * rows] = k_blocks[n][...]
    for c in range(GROUP // 2):
        q2 = jnp.concatenate([q[:, s] for s in pair(c)], 0)
        g2 = jnp.concatenate([g[:, s] for s in pair(c)], 0)
        b = bias[...]
        t = dot(k[...], q2, NT) * (scale * math.log2(math.e)) + jnp.concatenate([b, b], 1)
        p = jnp.exp2(t - jnp.max(t, axis=0, keepdims=True))
        p = (p * (1.0 / jnp.sum(p, axis=0, keepdims=True))).astype(jnp.bfloat16)
        probs[0, :, 2 * c * HEAD_DIM : (2 * c + 2) * HEAD_DIM] = p
        dv_c = dot(p, g2, NN)
        if c == 0:
            total[...] = dv_c
        else:
            total[...] += dv_c
    for n, owner in enumerate(owners_of(n_ctx)):
        dv[owner] = total[n * rows : (n + 1) * rows].astype(jnp.bfloat16)


def grads_kernel(q, g, probs, *refs):
    n_ctx = len(DISTANCES)
    k_blocks, v_blocks = refs[:n_ctx], refs[n_ctx : 2 * n_ctx]
    out, dq = refs[2 * n_ctx : 2 * n_ctx + 2]
    dk, (v, k_t, v_t, total) = refs[2 * n_ctx + 2 : 3 * n_ctx + 2], refs[3 * n_ctx + 2 :]
    rows = q.shape[0]
    scale = HEAD_DIM**-0.5
    for n in range(n_ctx):
        at = slice(n * rows, (n + 1) * rows)
        v[at] = v_blocks[n][...]
        k_t[:, at] = k_blocks[n][...].T
        v_t[:, at] = v_blocks[n][...].T
    for c in range(GROUP // 2):
        q2 = jnp.concatenate([q[:, s] for s in pair(c)], 0)
        g2 = jnp.concatenate([g[:, s] for s in pair(c)], 0)
        p = probs[0, :, 2 * c * HEAD_DIM : (2 * c + 2) * HEAD_DIM]
        out_t = dot(v_t[...], p, NN)
        g_t = g2.T
        delta = jnp.sum(g_t.astype(jnp.float32) * out_t, axis=0, keepdims=True)
        dots = dot(v[...], g_t, NN)
        slopes = (p.astype(jnp.float32) * (dots - delta)).astype(jnp.bfloat16)
        dq_t = dot(k_t[...], slopes, NN) * scale
        dk_c = dot(slopes, q2, NN)
        if c == 0:
            total[...] = dk_c
        else:
            total[...] += dk_c
        o2 = out_t.T.astype(jnp.bfloat16)
        d2 = dq_t.T.astype(jnp.bfloat16)
        for i, s in enumerate(pair(c)):
            out[:, s] = o2[i * HEAD_DIM : (i + 1) * HEAD_DIM]
            dq[:, s] = d2[i * HEAD_DIM : (i + 1) * HEAD_DIM]
    for n in range(n_ctx):
        dk[n][...] = (total[n * rows : (n + 1) * rows] * scale).astype(jnp.bfloat16)


def specs_of(rows, n_ctx):
    wide = pl.BlockSpec((rows, GROUP * HEAD_DIM), lambda h: (0, h))
    first = pl.BlockSpec((rows, HEAD_DIM), lambda h: (0, h))
    second = pl.BlockSpec((rows, HEAD_DIM), lambda h: (0, h + KV_HEADS))
    keys, values = [first] * n_ctx, [second] * (n_ctx - 1) + [first]
    parts = pl.BlockSpec((n_ctx, rows, HEAD_DIM), lambda h: (0, 0, h))
    square = pl.BlockSpec((1, n_ctx * rows, GROUP * rows), lambda h: (h, 0, 0))
    return wide, keys, values, parts, square


def probs_and_dv(q, g, k_blocks, lens, prefix, order):
    rows, n_ctx = q.shape[0], len(k_blocks)
    kv_width, total = k_blocks[-1].shape[1], rows * n_ctx
    wide, keys, values, parts, square = specs_of(rows, n_ctx)
    shape = jax.ShapeDtypeStruct
    return pl.pallas_call(
        probs_kernel,
        grid=(KV_HEADS,),
        in_specs=[pl.BlockSpec(memory_space=pltpu.SMEM)] * 3 + [wide, wide] + keys,
        out_specs=[square, parts],
        out_shape=[
            shape((KV_HEADS, total, GROUP * rows), jnp.bfloat16),
            shape((n_ctx, rows, kv_width), jnp.bfloat16),
        ],
        scratch_shapes=[
            pltpu.VMEM((total, rows), jnp.float32),
            pltpu.VMEM((total, HEAD_DIM), jnp.bfloat16),
            pltpu.VMEM((total, HEAD_DIM), jnp.float32),
        ],
        compiler_params=pltpu.CompilerParams(vmem_limit_bytes=VMEM),
        cost_estimate=pl.CostEstimate(
            flops=4 * HEADS * rows * total * HEAD_DIM, bytes_accessed=12 << 20, transcendentals=HEADS * rows * total
        ),
    )(lens, prefix, order, q, g, *k_blocks)


def out_and_grads(q, g, probs, k_blocks, v_blocks):
    rows, n_ctx = q.shape[0], len(k_blocks)
    kv_width, total = k_blocks[-1].shape[1], rows * n_ctx
    wide, keys, values, parts, square = specs_of(rows, n_ctx)
    shape = jax.ShapeDtypeStruct
    return pl.pallas_call(
        grads_kernel,
        grid=(KV_HEADS,),
        in_specs=[wide, wide, square] + keys + values,
        out_specs=[wide, wide] + [keys[0]] * n_ctx,
        out_shape=[shape(q.shape, jnp.bfloat16)] * 2 + [shape((rows, kv_width), jnp.bfloat16)] * n_ctx,
        scratch_shapes=[
            pltpu.VMEM((total, HEAD_DIM), jnp.bfloat16),
            pltpu.VMEM((HEAD_DIM, total), jnp.bfloat16),
            pltpu.VMEM((HEAD_DIM, total), jnp.bfloat16),
            pltpu.VMEM((total, HEAD_DIM), jnp.float32),
        ],
        compiler_params=pltpu.CompilerParams(vmem_limit_bytes=VMEM),
        cost_estimate=pl.CostEstimate(
            flops=8 * HEADS * rows * total * HEAD_DIM, bytes_accessed=14 << 20, transcendentals=0
        ),
    )(q, g, probs, *k_blocks, *v_blocks)


def along_ctx(a, far):
    n = lax.axis_size("ctx")
    return lax.ppermute(a, "ctx", [(i, (i + far) % n) for i in range(n)])


def plus(a, b):
    return (a.astype(jnp.float32) + b.astype(jnp.float32)).astype(jnp.bfloat16)


def place_of(i):
    return i >> 3, (i >> 1) & 3, i & 1


def index_of(y, x, core):
    return ((y % N_Y) * N_X + x % N_X) * 2 + core


def along_dp(a, dy, dx, other_core):
    pairs = []
    for i in range(lax.axis_size("dp")):
        y, x, core = place_of(i)
        pairs.append((i, index_of(y + dy, x + dx, core ^ other_core)))
    return lax.ppermute(a, "dp", pairs)


def over_x(pieces):
    return [pieces[0]] + [along_dp(pieces[d], 0, d if d < 3 else -1, 0) for d in range(1, N_X)]


def turn_kernel(where, *refs):
    targets = refs[2 * N_X :]
    for d in range(N_X):
        targets[d][0] = refs[d][...].T
        targets[d][1] = refs[N_X + d][...].T


def columns_for_x(layer, y, x, core):
    rows, model = layer.shape
    width = model // (N_X * N_Y * 2)

    def place(j, at, d):
        return (lax.rem(at[0] + j, N_Y) * N_X + lax.rem(at[1] + d, N_X)) * 2

    def mine(d):
        return pl.BlockSpec((rows, width), lambda j, at: (0, place(j, at, d) + at[2]))

    def other(d):
        return pl.BlockSpec((rows, width), lambda j, at: (0, place(j, at, d) + 1 - at[2]))

    return pl.pallas_call(
        turn_kernel,
        grid_spec=pltpu.PrefetchScalarGridSpec(
            num_scalar_prefetch=1,
            grid=(N_Y,),
            in_specs=[mine(d) for d in range(N_X)] + [other(d) for d in range(N_X)],
            out_specs=[pl.BlockSpec((2, width, rows), lambda j, at: (0, j, 0))] * N_X,
        ),
        out_shape=[jax.ShapeDtypeStruct((2, N_Y * width, rows), layer.dtype)] * N_X,
        cost_estimate=pl.CostEstimate(flops=0, bytes_accessed=4 * layer.size, transcendentals=0),
    )(jnp.stack([y, x, core]).astype(jnp.int32), *[layer] * (2 * N_X))


def weight_kernel(*refs):
    columns, (others, last_others, near, far, own), sent = refs[:N_X], refs[N_X : N_X + 5], refs[N_X + 5 :]
    rows = own.shape[0]
    tokens = near.shape[0] // N_X
    both = [
        jnp.concatenate([near[d * tokens : (d + 1) * tokens], far[d * tokens : (d + 1) * tokens]], 0) for d in range(N_X)
    ]
    for j in range(N_Y):
        at = slice(j * rows, (j + 1) * rows)
        away = [others[0, at], others[1, at], last_others[at], others[2, at]]
        pairs = [jnp.concatenate([columns[d][0, at], away[d]], 1) for d in range(N_X)]
        term = sum(dot(pairs[d], both[d], NN) for d in range(N_X))
        if j == 0:
            own[...] = term
        else:
            sent[j - 1][...] = term.astype(jnp.bfloat16)


def weight_terms(columns, others, last_others, near, far):
    rows, width = columns[0].shape[1] // N_Y, near.shape[1]
    shape = jax.ShapeDtypeStruct
    halves = pl.BlockSpec((1,) + columns[0].shape[1:], lambda i: (0, 0, 0))
    whole = [pl.BlockSpec(a.shape, lambda i, n=a.ndim: (0,) * n) for a in (others, last_others, near, far)]
    part = pl.BlockSpec((rows, width), lambda i: (0, 0))
    own, *sent = pl.pallas_call(
        weight_kernel,
        grid=(1,),
        in_specs=[halves] * N_X + whole,
        out_specs=[part] * N_Y,
        out_shape=[shape((rows, width), jnp.float32)] + [shape((rows, width), jnp.bfloat16)] * (N_Y - 1),
        compiler_params=pltpu.CompilerParams(vmem_limit_bytes=VMEM // 4),
        cost_estimate=pl.CostEstimate(flops=0, bytes_accessed=1 << 16, transcendentals=0),
    )(*columns, others, last_others, near, far)
    return own, sent


def on_device(layer_input, query, key, value, grad_out, doc_lengths, prefix_lengths, stretch_order):
    n_ctx = lax.axis_size("ctx")
    y, x, core = place_of(lax.axis_index("dp"))
    here = jnp.concatenate([key[0], value[0]], 1)
    half = n_ctx // 2
    width = key.shape[2]
    up, down = [here], [here]
    columns = columns_for_x(layer_input[0], y, x, core)
    moved = over_x(columns)
    for step in range(half - 1):
        if step == 1:
            up[1], down[1], picked = lax.optimization_barrier((up[1], down[1], columns[0]))
        up.append(along_ctx(up[-1], 1))
        down.append(along_ctx(down[-1], -1))
    far_key = along_ctx(up[-1][:, :width], 1)
    far_value = along_ctx(down[-1][:, width:], -1)
    far_key, far_value, moved[1], moved[3] = lax.optimization_barrier((far_key, far_value, moved[1], moved[3]))
    blocks = [down[far] if far > 0 else up[-far] for far in DISTANCES[:-1]]
    keys, values = blocks + [far_key], blocks + [far_value]

    q, g = query[0], grad_out[0]
    probs, dv = probs_and_dv(q, g, keys, doc_lengths, prefix_lengths, stretch_order)
    got = lax.all_to_all(dv, "ctx", split_axis=0, concat_axis=0, tiled=True)
    moved[0] = picked
    early = jnp.stack([moved[d][1] for d in (0, 1, 3)])
    probs, early = lax.optimization_barrier((probs, early))
    others = along_dp(early, 0, 0, 1)
    out, dq, *parts = out_and_grads(q, g, probs, keys, values)
    parts = dict(zip(DISTANCES, parts))
    moved[2], parts[half] = lax.optimization_barrier((moved[2], parts[half]))
    last_others = along_dp(moved[2][1], 0, 0, 1)

    rising = along_ctx(parts[half], 1)
    got, rising = lax.optimization_barrier((got, rising))
    grad_value = jnp.sum(got.astype(jnp.float32), axis=0).astype(jnp.bfloat16)
    rising, falling = along_ctx(plus(rising, parts[half - 1]), 1), along_ctx(parts[1 - half], -1)

    near = jnp.concatenate(over_x([grad_value] * N_X), 0)
    near, rising, falling = lax.optimization_barrier((near, rising, falling))
    far = along_dp(near, 0, 0, 1)
    rising, falling = plus(rising, parts[half - 2]), plus(falling, parts[2 - half])
    rising, falling = along_ctx(rising, 1), along_ctx(falling, -1)
    own, sent = weight_terms(moved, others, last_others, near, far)
    total = own
    for d in range(1, N_Y):
        total = total + along_dp(sent[d - 1], d if d < 3 else -1, 0, 0).astype(jnp.float32)
    total = total.astype(jnp.bfloat16).reshape(n_ctx, -1, near.shape[1])
    total, rising, falling = lax.optimization_barrier((total, rising, falling))
    rising, falling = plus(rising, parts[half - 3]), plus(falling, parts[3 - half])
    rising, falling = along_ctx(rising, 1), along_ctx(falling, -1)

    grad_key = plus(plus(rising, falling), parts[0])
    last = lax.all_to_all(total, "ctx", split_axis=0, concat_axis=0, tiled=True)
    weight = jnp.sum(last.astype(jnp.float32), axis=0)
    return (out[None], dq[None], grad_key[None], weight)


def solution(mesh):
    rows = P("dp", "ctx", None)
    scalars = P("dp", None)
    return jax.shard_map(
        on_device,
        mesh=mesh,
        in_specs=(rows,) * 5 + (scalars,) * 3,
        out_specs=(rows, rows, rows, P(("dp", "ctx"), None)),
        check_vma=False,
    )
```
